32 devices in a mesh: dom: 2 (over y), grp: 4 (over x, core), tp: 4 (over z).
Axes of the slice: x: 2, y: 2, z: 4, core: 2. Of those that a mesh axis runs over, the one named last changes fastest.
Arguments:
- hidden: bfloat16 [32, 128, 16384], P(('dom', 'grp'), None, 'tp'), parts along dimension 0
- norm_gain: float32 [16384], P('tp'), may hold values from 0.1 to 1.9
- kv_weight: bfloat16 [16384, 8, 256], P('tp'), may hold values from -0.046875 to 0.046875
- dest_slot: int32 [32], P(('dom', 'grp')), parts along dimension 0, may hold values from -1 to 7, as said below
- session_len: int32 [8], P(('dom', 'grp')), parts along dimension 0, may hold values from 129 to 256
- session_start: int32 [8], P(('dom', 'grp')), parts along dimension 0, may hold values from 0 to 16383
Outputs:
- kv_cache: bfloat16 [16, 128, 8, 256], P(('dom', 'grp'), None, 'tp'), parts along dimension 0
The draws below stay inside these ranges and needn't reach their ends.
There are 2 independent parts, one for each index of `dom`. The reference program is written for one: setup_inputs(seed, part) draws one part's arguments, and reference() takes and returns one part's arrays. A program takes and returns all parts, laid end to end along the dimension named above; an argument that names none is the same for every part. Nothing has to cross between parts.
Inputs may be any that keep to these rules, and one draw needn't show every extreme that they name: `dest_slot`: each of the 8 cache blocks is named by exactly one stored slot; the blocks of one owner come from different groups, so a group sends at most one block to each owner; a group stores at most 4 blocks and some group stores exactly 4; -1 marks an empty slot.
All inputs are finite; a program needn't handle non-finite values.
Results may differ from the reference program's by a relative error of at most 0.013.
Values may be sent and summed in bfloat16 or wider, within the bound.
A program may use at most 128 MiB of HBM per device.

```python
import jax
import jax.numpy as jnp
from jax import lax

D = 16384
KVH = 8
HD = 128
BLK = 128
MAXPOS = 16384
OWN_BLK = 2
SLOTS = 4
STORE = 16
CACHE = 8
N_GRP = 4
N_TP = 4


def draw_hidden(key, part):
    key = jax.random.fold_in(key, 5)
    key_rows, key_cols, key_noise = jax.random.split(key, 3)
    place = jnp.arange(D).astype(jnp.float32) / (D - 1)
    rough = jnp.exp(jax.random.uniform(key_cols, (1, 1, D), jnp.float32, -0.5, 0.5))
    rows = jnp.exp(jax.random.uniform(key_rows, (STORE, BLK, 1), jnp.float32, jnp.log(0.3), jnp.log(3.0)))
    noise = jax.random.normal(key_noise, (STORE, BLK, D), jnp.float32)
    ramp = jnp.exp(jnp.log(0.6) + jnp.log(2.5) * place)
    cols = rough * ramp[None, None, :]
    return (noise * rows * cols).astype(jnp.bfloat16)


def draw_dest_slot(key, part):
    key = jax.random.fold_in(key, 11)
    key_src, key_own, key_slot = jax.random.split(key, 3)
    blocks = jnp.arange(CACHE).astype(jnp.int32)
    owner = blocks // OWN_BLK
    inner = blocks % OWN_BLK
    leading = OWN_BLK - OWN_BLK // 3
    offset = jnp.where(inner < leading, inner, N_GRP // 2 + inner - leading)
    source = (owner // 2 + offset) % N_GRP
    same = source[:, None] == source[None, :]
    earlier = blocks[None, :] < blocks[:, None]
    rank = jnp.sum((same & earlier).astype(jnp.int32), axis=1)
    src_label = jax.random.permutation(key_src, N_GRP)[source]
    own_label = jax.random.permutation(key_own, N_GRP)[owner]
    scores = jax.random.randint(key_slot, (N_GRP, SLOTS), 0, 1 << 20) * SLOTS + jnp.arange(SLOTS)[None, :]
    slot_order = jnp.argsort(scores, axis=1).astype(jnp.int32)
    slot = slot_order[src_label, rank]
    empty = jnp.full((STORE,), -1, jnp.int32)
    return empty.at[src_label * SLOTS + slot].set((own_label * OWN_BLK + inner).astype(jnp.int32))


def plant(array, stream_key, least, high):
    dims = array.shape
    index_at = [jax.random.randint(jax.random.fold_in(stream_key, axis), (), 0, dims[axis]) for axis in range(len(dims))]
    array = array.at[tuple(index_at)].set(least)
    longest = dims.index(max(dims))
    index_at[longest] = (index_at[longest] + 1) % dims[longest]
    return array.at[tuple(index_at)].set(high)


def block_levels(rng, extent, pieces, smallest, largest):
    def one(position, shards_of):
        draws = jax.random.uniform(jax.random.fold_in(jax.random.fold_in(rng, 6), position), (shards_of,), jnp.float32, smallest / len(pieces), largest / len(pieces))
        return jnp.repeat(jnp.exp(draws), extent[position] // shards_of).reshape((-1,) + (1,) * (len(extent) - position - 1))

    gain = one(*pieces[0])
    for cut in pieces[1:]:
        gain = gain * one(*cut)
    return gain


def gaussian(stream_key, shape, scale, reach, cuts=(), held_as=jnp.bfloat16):
    drawn = scale * jax.random.normal(stream_key, shape, jnp.float32)
    if cuts:
        drawn = drawn * block_levels(stream_key, shape, cuts, -0.22, 0.18)
    return jnp.clip(drawn, -reach, reach).astype(held_as)


def setup_inputs(seed: int = 0, part: int = 0) -> dict:
    seeds = jax.random.split(jax.random.key(seed), 7)
    part_keys = jax.random.split(jax.random.fold_in(seeds[6], part), 7)
    return {
        "hidden": draw_hidden(jax.random.fold_in(jax.random.fold_in(seeds[6], part), 71), part),
        "norm_gain": jnp.clip(1.0 + 0.18 * jax.random.normal(seeds[1], (D,), jnp.float32), 0.1, 1.9),
        "kv_weight": gaussian(seeds[2], (D, KVH, 2 * HD), D ** -0.5, 0.046875, ((0, 4),)),
        "dest_slot": draw_dest_slot(jax.random.fold_in(jax.random.fold_in(seeds[6], part), 71), part),
        "session_len": plant(jax.random.randint(part_keys[4], (N_GRP,), (OWN_BLK - 1) * BLK + 1, OWN_BLK * BLK + 1), jax.random.fold_in(part_keys[4], 1), (OWN_BLK - 1) * BLK + 1, OWN_BLK * BLK).astype(jnp.int32),
        "session_start": plant(jax.random.randint(part_keys[5], (N_GRP,), 0, MAXPOS), jax.random.fold_in(part_keys[5], 1), 0, MAXPOS - 1).astype(jnp.int32),
    }


def rotate_keys(kv, positions):
    half = HD // 2
    steps = jnp.arange(half).astype(jnp.float32)
    freqs = jnp.exp(-jnp.log(jnp.float32(500000.0)) * (2.0 * steps / HD))
    angles = positions.astype(jnp.float32)[:, None] * freqs[None, :]
    cosine = jnp.cos(angles)[:, None, :]
    sine = jnp.sin(angles)[:, None, :]
    first = kv[..., :half]
    second = kv[..., half:HD]
    keys = jnp.concatenate([first * cosine - second * sine, second * cosine + first * sine], axis=-1)
    return jnp.concatenate([keys, kv[..., HD:]], axis=-1)

def reference(hidden, norm_gain, kv_weight, dest_slot, session_len, session_start):
    width_local = D // N_TP
    cache_ids = jnp.arange(CACHE).astype(jnp.int32)
    match = dest_slot[None, :] == cache_ids[:, None]
    stored = lax.optimization_barrier(jnp.sum(jnp.where(match, jnp.arange(STORE).astype(jnp.int32)[None, :], 0), axis=1)).astype(jnp.int32)
    weight = kv_weight.astype(jnp.float32).reshape(N_TP, width_local, KVH * 2 * HD)
    tokens = jnp.arange(BLK).astype(jnp.int32)

    def restore(cache_id):
        index = stored[cache_id]
        block = lax.dynamic_index_in_dim(hidden, index, 0, keepdims=False).astype(jnp.float32)
        owner = cache_id // OWN_BLK
        inner = cache_id % OWN_BLK
        scaled = lax.optimization_barrier((block * norm_gain[None, :]).astype(jnp.bfloat16)).astype(jnp.float32)
        parts = jnp.einsum('bnd,nde->nbe', scaled.reshape(BLK, N_TP, width_local), weight)
        raw = lax.optimization_barrier(jnp.sum(parts.astype(jnp.bfloat16).astype(jnp.float32), axis=0))
        inv = lax.rsqrt(lax.optimization_barrier(jnp.sum(block * block, axis=1)) / D + 1e-05)
        kv = (raw * inv[:, None]).reshape(BLK, KVH, 2 * HD)
        offsets = inner * BLK + tokens
        positions = session_start[owner] + offsets
        live = offsets < session_len[owner]
        rotated = rotate_keys(kv, positions)
        return jnp.where(live[:, None, None], rotated, 0.0).astype(jnp.bfloat16)
    return lax.map(restore, cache_ids)
```

```python
import functools

import jax
import jax.numpy as jnp
from jax import lax
from jax.experimental import pallas as pl
from jax.experimental.pallas import tpu as pltpu
from jax.sharding import PartitionSpec as P

HD = 128
epsilon = 1e-05
MESH = pl.DeviceIdType.MESH


def exchange_kernel(
    groups, tps, own, heads, width,
    dest_ref, len_ref, part_ref, ss_ref, cos_ref, sin_ref,
    out_ref,
    sent, got, mixed, final, meta_s, meta_r, sums_s, sums_r,
    s_send, s_recv, c_send, c_recv, m_send, m_recv, q_send, q_recv,
):
    g = lax.axis_index("grp")
    z = lax.axis_index("tp")
    slots = part_ref.shape[1]
    blk = part_ref.shape[2]
    wide = part_ref.shape[3]

    def over(n, body):
        lax.fori_loop(0, n, lambda i, c: (body(i), c)[1], 0)

    def grp_peer(k):
        return lax.rem(g + k + 1, groups)

    def tp_peer(k):
        return lax.rem(z + k + 1, tps)

    barrier = pltpu.get_barrier_semaphore()

    @functools.partial(over, groups - 1)
    def _(k):
        pl.semaphore_signal(barrier, inc=1, device_id={"grp": grp_peer(k)}, device_id_type=MESH)

    @functools.partial(over, tps - 1)
    def _(k):
        pl.semaphore_signal(barrier, inc=1, device_id={"tp": tp_peer(k)}, device_id_type=MESH)

    def slot_of(owner):
        index, code = jnp.int32(0), jnp.int32(0)
        for s in range(slots):
            inner = dest_ref[s] - owner * own
            hit = (inner >= 0) & (inner < own)
            index = jnp.where(hit, s, index)
            code = jnp.where(hit, inner + 1, code)
        return index, code

    rows8 = lax.broadcasted_iota(jnp.int32, (8, wide), 0)

    def meta_of(owner):
        index, code = slot_of(owner)
        squares = jnp.broadcast_to(ss_ref[index], (8, wide))
        marks = jnp.full((8, wide), code.astype(jnp.float32))
        return jnp.where(rows8 == 0, squares, marks)

    def block_copy(t, o, src_g):
        return pltpu.make_async_remote_copy(
            src_ref=sent.at[t, o], dst_ref=got.at[t, src_g],
            send_sem=s_send.at[t, o], recv_sem=s_recv.at[t, src_g],
            device_id={"grp": o}, device_id_type=MESH,
        )

    def meta_copy(o, src_g):
        return pltpu.make_async_remote_copy(
            src_ref=meta_s.at[o], dst_ref=meta_r.at[src_g],
            send_sem=m_send.at[o], recv_sem=m_recv.at[src_g],
            device_id={"grp": o}, device_id_type=MESH,
        )

    def shard_copy(t, src_z):
        return pltpu.make_async_remote_copy(
            src_ref=mixed.at[t], dst_ref=final.at[src_z],
            send_sem=c_send.at[t], recv_sem=c_recv.at[src_z],
            device_id={"tp": t}, device_id_type=MESH,
        )

    def sums_copy(t, src_z):
        return pltpu.make_async_remote_copy(
            src_ref=sums_s, dst_ref=sums_r.at[src_z],
            send_sem=q_send.at[t], recv_sem=q_recv.at[src_z],
            device_id={"tp": t}, device_id_type=MESH,
        )

    meta_r[g] = meta_of(g)

    @functools.partial(over, groups - 1)
    def _(k):
        o = grp_peer(k)
        meta_s[o] = meta_of(o)

    pl.semaphore_wait(barrier, groups + tps - 2)

    @functools.partial(over, groups - 1)
    def _(k):
        meta_copy(grp_peer(k), g).start()

    @functools.partial(over, tps)
    def _(i):
        t = tp_peer(i)

        @functools.partial(over, groups - 1)
        def _(k):
            o = grp_peer(k)
            index, _ = slot_of(o)
            for h in range(heads):
                sent[t, o, h] = part_ref[t * heads + h, index]
            block_copy(t, o, g).start()

        mine, _ = slot_of(g)
        for h in range(heads):
            got[t, g, h] = part_ref[t * heads + h, mine]

    @functools.partial(over, groups - 1)
    def _(k):
        o = grp_peer(k)
        meta_copy(o, o).wait_recv()

    def add_squares(s, total):
        marks = jnp.broadcast_to(meta_r[s, 1:2, :], (8, wide))
        squares = jnp.broadcast_to(meta_r[s, 0:1, :], (8, wide))
        return total + jnp.where(marks == (rows8 + 1).astype(jnp.float32), squares, 0.0)

    sums = lax.fori_loop(0, groups, add_squares, jnp.zeros((8, wide), jnp.float32))
    sums_s[...] = sums

    @functools.partial(over, tps - 1)
    def _(i):
        sums_copy(tp_peer(i), z).start()

    def mix(t):
        @functools.partial(over, groups - 1)
        def _(k):
            o = grp_peer(k)
            block_copy(t, o, o).wait_recv()

        for j in range(own):
            for h in range(heads):
                def pick(s, total):
                    marks = jnp.broadcast_to(meta_r[s, 1:2, :], (blk, wide))
                    block = got[t, s, h].astype(jnp.float32)
                    return total + jnp.where(marks == float(j + 1), block, 0.0)

                picked = lax.fori_loop(0, groups, pick, jnp.zeros((blk, wide), jnp.float32))
                mixed[t, j, h] = picked.astype(jnp.bfloat16)

    @functools.partial(over, tps - 1)
    def _(i):
        t = tp_peer(i)
        mix(t)
        shard_copy(t, z).start()

    mix(z)

    @functools.partial(over, tps - 1)
    def _(i):
        t = tp_peer(i)
        sums_copy(t, t).wait_recv()

    def add_sums(i, total):
        return total + sums_r[tp_peer(i)]

    total = lax.fori_loop(0, tps - 1, add_sums, sums)
    inverse = lax.rsqrt(total[:, :blk] / (width * tps) + epsilon)

    @functools.partial(over, tps - 1)
    def _(i):
        t = tp_peer(i)
        shard_copy(t, t).wait_recv()

    half = HD // 2
    token = lax.broadcasted_iota(jnp.int32, (blk, HD), 0)
    length = len_ref[0]
    for j in range(own):
        scale = jnp.transpose(jnp.broadcast_to(inverse[j : j + 1, :], (blk, blk)))
        live = token + j * blk < length
        for h in range(heads):
            def add(i, total):
                return total + final[tp_peer(i), j, h].astype(jnp.float32)

            raw = lax.fori_loop(0, tps - 1, add, mixed[z, j, h].astype(jnp.float32))
            key = raw[:, :HD] * scale
            value = raw[:, HD:] * scale
            swapped = pltpu.roll(key, half, 1)
            turned = key * cos_ref[j] + swapped * sin_ref[j]
            out_ref[j, h, :, :HD] = jnp.where(live, turned, 0.0).astype(out_ref.dtype)
            out_ref[j, h, :, HD:] = jnp.where(live, value, 0.0).astype(out_ref.dtype)

    @functools.partial(over, groups - 1)
    def _(k):
        o = grp_peer(k)
        meta_copy(o, g).wait_send()

    @functools.partial(over, tps)
    def _(t):
        @functools.partial(over, groups - 1)
        def _(k):
            block_copy(t, grp_peer(k), g).wait_send()

    @functools.partial(over, tps - 1)
    def _(i):
        t = tp_peer(i)
        sums_copy(t, z).wait_send()
        shard_copy(t, z).wait_send()


def rotation(start, own, blk):
    half = HD // 2
    steps = jnp.arange(half).astype(jnp.float32)
    freqs = jnp.exp(-jnp.log(jnp.float32(500000.0)) * (2.0 * steps / HD))
    positions = start[0] + jnp.arange(own * blk)
    angles = positions.astype(jnp.float32)[:, None] * freqs[None, :]
    cosine, sine = jnp.cos(angles), jnp.sin(angles)
    return (
        jnp.concatenate([cosine, cosine], axis=1).reshape(own, blk, HD),
        jnp.concatenate([-sine, sine], axis=1).reshape(own, blk, HD),
    )


def body(hidden, norm_gain, kv_weight, dest_slot, session_len, session_start):
    groups, tps = lax.axis_size("grp"), lax.axis_size("tp")
    slots, blk, width = hidden.shape
    own = (3 * groups + 7) // 8
    heads = kv_weight.shape[1] // tps
    wide_cols = kv_weight.shape[2]
    cosine, sine = rotation(session_start, own, blk)
    wide = hidden.astype(jnp.float32)
    squares = jnp.sum(wide * wide, axis=2)
    squares = jnp.concatenate([squares, squares], axis=1)[:, None, :]
    scaled = (wide * norm_gain[None, None, :]).astype(jnp.bfloat16).reshape(slots * blk, width)
    parts = jnp.einsum("rd,dhe->hre", scaled, kv_weight, preferred_element_type=jnp.float32)
    parts = parts.astype(jnp.bfloat16).reshape(kv_weight.shape[1], slots, blk, wide_cols)
    vmem = pl.BlockSpec(memory_space=pltpu.VMEM)
    smem = pl.BlockSpec(memory_space=pltpu.SMEM)
    shard = (heads, blk, wide_cols)
    dma = pltpu.SemaphoreType.DMA
    out = pl.pallas_call(
        functools.partial(exchange_kernel, groups, tps, own, heads, width),
        out_shape=jax.ShapeDtypeStruct((own,) + shard, jnp.bfloat16),
        in_specs=[smem, smem, vmem, vmem, vmem, vmem],
        out_specs=vmem,
        scratch_shapes=[
            pltpu.VMEM((tps, groups) + shard, jnp.bfloat16),
            pltpu.VMEM((tps, groups) + shard, jnp.bfloat16),
            pltpu.VMEM((tps, own) + shard, jnp.bfloat16),
            pltpu.VMEM((tps, own) + shard, jnp.bfloat16),
            pltpu.VMEM((groups, 8, wide_cols), jnp.float32),
            pltpu.VMEM((groups, 8, wide_cols), jnp.float32),
            pltpu.VMEM((8, wide_cols), jnp.float32),
            pltpu.VMEM((tps, 8, wide_cols), jnp.float32),
            dma((tps, groups)), dma((tps, groups)),
            dma((tps,)), dma((tps,)),
            dma((groups,)), dma((groups,)),
            dma((tps,)), dma((tps,)),
        ],
        compiler_params=pltpu.CompilerParams(
            collective_id=0, has_side_effects=True, vmem_limit_bytes=40 * 1024 * 1024
        ),
        name="exchange",
    )(dest_slot, session_len, parts, squares, cosine, sine)
    return jnp.transpose(out, (0, 2, 1, 3))


def solution(mesh):
    in_specs = (
        P(("dom", "grp"), None, "tp"),
        P("tp"),
        P("tp", None, None),
        P(("dom", "grp")),
        P(("dom", "grp")),
        P(("dom", "grp")),
    )
    out_specs = P(("dom", "grp"), None, "tp", None)
    return jax.shard_map(body, mesh=mesh, in_specs=in_specs, out_specs=out_specs, check_vma=False)
```

```python
import functools

import jax
import jax.numpy as jnp
from jax import lax
from jax.experimental import pallas as pl
from jax.experimental.pallas import tpu as pltpu
from jax.sharding import PartitionSpec as P

HD = 128
epsilon = 1e-05
MESH = pl.DeviceIdType.MESH


def exchange_kernel(
    groups, tps, own, heads, width,
    dest_ref, len_ref, part_ref, hidden_ref, cos_ref, sin_ref,
    out_ref,
    sent, got, mixed, final, mark_s, mark_r, square_s, square_r, sums_s, sums_r, slot_sums, scales,
    s_send, s_recv, c_send, c_recv, m_send, m_recv, r_send, r_recv, q_send, q_recv,
):
    g = lax.axis_index("grp")
    z = lax.axis_index("tp")
    slots = part_ref.shape[1]
    blk = part_ref.shape[2]
    wide = part_ref.shape[3]
    units = sent.shape[1]
    cuts = units // heads
    rows = blk // cuts

    def over(n, body):
        lax.fori_loop(0, n, lambda i, c: (body(i), c)[1], 0)

    def grp_peer(k):
        return lax.rem(g + k + 1, groups)

    def tp_peer(k):
        side = lax.div(k + 1, 2) * (2 * lax.rem(k, 2) - 1)
        return lax.rem(z + tps // 2 + side, tps)

    barrier = pltpu.get_barrier_semaphore()

    @functools.partial(over, groups - 1)
    def _(k):
        pl.semaphore_signal(barrier, inc=1, device_id={"grp": grp_peer(k)}, device_id_type=MESH)

    @functools.partial(over, tps - 1)
    def _(k):
        pl.semaphore_signal(barrier, inc=1, device_id={"tp": tp_peer(k)}, device_id_type=MESH)

    def slot_of(owner):
        index, code = jnp.int32(0), jnp.int32(0)
        for s in range(slots):
            inner = dest_ref[s] - owner * own
            hit = (inner >= 0) & (inner < own)
            index = jnp.where(hit, s, index)
            code = jnp.where(hit, inner + 1, code)
        return index, code

    rows8 = lax.broadcasted_iota(jnp.int32, (8, wide), 0)

    def mark_of(owner):
        _, code = slot_of(owner)
        return jnp.full((8, wide), code.astype(jnp.float32))

    def block_copy(t, u, o, src_g):
        return pltpu.make_async_remote_copy(
            src_ref=sent.at[t, u, o], dst_ref=got.at[t, u, src_g],
            send_sem=s_send.at[t, u, o], recv_sem=s_recv.at[t, u, src_g],
            device_id={"grp": o}, device_id_type=MESH,
        )

    def mark_copy(o, src_g):
        return pltpu.make_async_remote_copy(
            src_ref=mark_s.at[o], dst_ref=mark_r.at[src_g],
            send_sem=m_send.at[o], recv_sem=m_recv.at[src_g],
            device_id={"grp": o}, device_id_type=MESH,
        )

    def square_copy(o, src_g):
        return pltpu.make_async_remote_copy(
            src_ref=square_s.at[o], dst_ref=square_r.at[src_g],
            send_sem=r_send.at[o], recv_sem=r_recv.at[src_g],
            device_id={"grp": o}, device_id_type=MESH,
        )

    def shard_copy(t, u, src_z):
        return pltpu.make_async_remote_copy(
            src_ref=mixed.at[t, u], dst_ref=final.at[src_z, u],
            send_sem=c_send.at[t, u], recv_sem=c_recv.at[src_z, u],
            device_id={"tp": t}, device_id_type=MESH,
        )

    def sums_copy(t, src_z):
        return pltpu.make_async_remote_copy(
            src_ref=sums_s, dst_ref=sums_r.at[src_z],
            send_sem=q_send.at[t], recv_sem=q_recv.at[src_z],
            device_id={"tp": t}, device_id_type=MESH,
        )

    mark_r[g] = mark_of(g)

    @functools.partial(over, groups - 1)
    def _(k):
        o = grp_peer(k)
        mark_s[o] = mark_of(o)

    pl.semaphore_wait(barrier, groups + tps - 2)

    @functools.partial(over, groups - 1)
    def _(k):
        mark_copy(grp_peer(k), g).start()

    mine, _ = slot_of(g)

    @functools.partial(over, tps)
    def _(i):
        t = tp_peer(i)

        @functools.partial(over, units)
        def _(u):
            head = t * heads + lax.div(u, cuts)
            span = pl.ds(pl.multiple_of(lax.rem(u, cuts) * rows, rows), rows)

            @functools.partial(over, groups - 1)
            def _(k):
                o = grp_peer(k)
                index, _ = slot_of(o)
                sent[t, u, o] = part_ref[head, index, span, :]
                block_copy(t, u, o, g).start()

            got[t, u, g] = part_ref[head, mine, span, :]

    @functools.partial(over, groups - 1)
    def _(k):
        o = grp_peer(k)
        mark_copy(o, o).wait_recv()

    def mix(t, u):
        @functools.partial(over, groups - 1)
        def _(k):
            o = grp_peer(k)
            block_copy(t, u, o, o).wait_recv()

        for j in range(own):
            def pick(s, total):
                marks = jnp.broadcast_to(mark_r[s, 0:1, :], (rows, wide))
                block = got[t, u, s].astype(jnp.float32)
                return total + jnp.where(marks == float(j + 1), block, 0.0)

            picked = lax.fori_loop(0, groups, pick, jnp.zeros((rows, wide), jnp.float32))
            mixed[t, u, j] = picked.astype(jnp.bfloat16)

    def mix_and_send(t):
        @functools.partial(over, units)
        def _(u):
            mix(t, u)
            shard_copy(t, u, z).start()

    mix_and_send(tp_peer(0))

    lanes = HD

    @functools.partial(over, slots)
    def _(s):
        for r in range(0, blk, 32):
            def add(c, total):
                span = pl.ds(pl.multiple_of(c * lanes, lanes), lanes)
                x = hidden_ref[s, r : r + 32, span].astype(jnp.float32)
                return total + x * x

            slot_sums[s, r : r + 32, :] = lax.fori_loop(
                0, width // lanes, add, jnp.zeros((32, lanes), jnp.float32)
            )

    def squares_of(owner):
        index, _ = slot_of(owner)
        line = jnp.sum(jnp.transpose(slot_sums[index]), axis=0, keepdims=True)
        return jnp.broadcast_to(jnp.concatenate([line, line], axis=1), (8, wide))

    square_r[g] = squares_of(g)

    @functools.partial(over, groups - 1)
    def _(k):
        o = grp_peer(k)
        square_s[o] = squares_of(o)
        square_copy(o, g).start()

    @functools.partial(over, groups - 1)
    def _(k):
        o = grp_peer(k)
        square_copy(o, o).wait_recv()

    def add_squares(s, total):
        same = mark_r[s] == (rows8 + 1).astype(jnp.float32)
        return total + jnp.where(same, square_r[s], 0.0)

    sums = lax.fori_loop(0, groups, add_squares, jnp.zeros((8, wide), jnp.float32))
    sums_s[...] = sums

    @functools.partial(over, tps - 1)
    def _(i):
        sums_copy(tp_peer(i), z).start()

    @functools.partial(over, tps - 2)
    def _(i):
        mix_and_send(tp_peer(i + 1))

    @functools.partial(over, units)
    def _(u):
        mix(z, u)

    @functools.partial(over, tps - 1)
    def _(i):
        t = tp_peer(i)
        sums_copy(t, t).wait_recv()

    def add_sums(i, total):
        return total + sums_r[tp_peer(i)]

    total = lax.fori_loop(0, tps - 1, add_sums, sums)
    inverse = lax.rsqrt(total[:, :blk] / (width * tps) + epsilon)

    half = HD // 2
    token = lax.broadcasted_iota(jnp.int32, (rows, HD), 0)
    length = len_ref[0]
    for j in range(own):
        scales[j] = jnp.transpose(jnp.broadcast_to(inverse[j : j + 1, :], (blk, blk)))

    @functools.partial(over, units)
    def _(u):
        @functools.partial(over, tps - 1)
        def _(i):
            t = tp_peer(i)
            shard_copy(t, u, t).wait_recv()

        head = lax.div(u, cuts)
        first = pl.multiple_of(lax.rem(u, cuts) * rows, rows)
        span = pl.ds(first, rows)
        for j in range(own):
            live = token + (j * blk + first) < length

            def add(i, total):
                return total + final[tp_peer(i), u, j].astype(jnp.float32)

            raw = lax.fori_loop(0, tps - 1, add, mixed[z, u, j].astype(jnp.float32))
            scale = scales[j, span, :]
            key = raw[:, :HD] * scale
            value = raw[:, HD:] * scale
            swapped = pltpu.roll(key, half, 1)
            turned = key * cos_ref[j, span, :] + swapped * sin_ref[j, span, :]
            out_ref[j, head, span, :HD] = jnp.where(live, turned, 0.0).astype(out_ref.dtype)
            out_ref[j, head, span, HD:] = jnp.where(live, value, 0.0).astype(out_ref.dtype)

    @functools.partial(over, groups - 1)
    def _(k):
        o = grp_peer(k)
        mark_copy(o, g).wait_send()
        square_copy(o, g).wait_send()

    @functools.partial(over, tps)
    def _(t):
        @functools.partial(over, units)
        def _(u):
            @functools.partial(over, groups - 1)
            def _(k):
                block_copy(t, u, grp_peer(k), g).wait_send()

    @functools.partial(over, tps - 1)
    def _(i):
        t = tp_peer(i)
        sums_copy(t, z).wait_send()

        @functools.partial(over, units)
        def _(u):
            shard_copy(t, u, z).wait_send()


def rotation(start, own, blk):
    half = HD // 2
    steps = jnp.arange(half).astype(jnp.float32)
    freqs = jnp.exp(-jnp.log(jnp.float32(500000.0)) * (2.0 * steps / HD))
    positions = start[0] + jnp.arange(own * blk)
    angles = positions.astype(jnp.float32)[:, None] * freqs[None, :]
    cosine, sine = jnp.cos(angles), jnp.sin(angles)
    return (
        jnp.concatenate([cosine, cosine], axis=1).reshape(own, blk, HD),
        jnp.concatenate([-sine, sine], axis=1).reshape(own, blk, HD),
    )


def body(hidden, norm_gain, kv_weight, dest_slot, session_len, session_start):
    groups, tps = lax.axis_size("grp"), lax.axis_size("tp")
    slots, blk, width = hidden.shape
    own = (3 * groups + 7) // 8
    heads = kv_weight.shape[1] // tps
    wide_cols = kv_weight.shape[2]
    cosine, sine = rotation(session_start, own, blk)
    wide = hidden.astype(jnp.float32)
    scaled = (wide * norm_gain[None, None, :]).astype(jnp.bfloat16).reshape(slots * blk, width)
    parts = jnp.einsum("rd,dhe->hre", scaled, kv_weight, preferred_element_type=jnp.float32)
    parts = parts.astype(jnp.bfloat16).reshape(kv_weight.shape[1], slots, blk, wide_cols)
    vmem = pl.BlockSpec(memory_space=pltpu.VMEM)
    smem = pl.BlockSpec(memory_space=pltpu.SMEM)
    cuts = 2
    units = heads * cuts
    piece = (blk // cuts, wide_cols)
    line = pltpu.VMEM((groups, 8, wide_cols), jnp.float32)
    dma = pltpu.SemaphoreType.DMA
    out = pl.pallas_call(
        functools.partial(exchange_kernel, groups, tps, own, heads, width),
        out_shape=jax.ShapeDtypeStruct((own, heads, blk, wide_cols), jnp.bfloat16),
        in_specs=[smem, smem, vmem, vmem, vmem, vmem],
        out_specs=vmem,
        scratch_shapes=[
            pltpu.VMEM((tps, units, groups) + piece, jnp.bfloat16),
            pltpu.VMEM((tps, units, groups) + piece, jnp.bfloat16),
            pltpu.VMEM((tps, units, own) + piece, jnp.bfloat16),
            pltpu.VMEM((tps, units, own) + piece, jnp.bfloat16),
            line, line, line, line,
            pltpu.VMEM((8, wide_cols), jnp.float32),
            pltpu.VMEM((tps, 8, wide_cols), jnp.float32),
            pltpu.VMEM((slots, blk, HD), jnp.float32),
            pltpu.VMEM((own, blk, HD), jnp.float32),
            dma((tps, units, groups)), dma((tps, units, groups)),
            dma((tps, units)), dma((tps, units)),
            dma((groups,)), dma((groups,)),
            dma((groups,)), dma((groups,)),
            dma((tps,)), dma((tps,)),
        ],
        compiler_params=pltpu.CompilerParams(
            collective_id=0, has_side_effects=True, vmem_limit_bytes=40 * 1024 * 1024
        ),
        name="exchange",
    )(dest_slot, session_len, parts, hidden, cosine, sine)
    return jnp.transpose(out, (0, 2, 1, 3))


def solution(mesh):
    in_specs = (
        P(("dom", "grp"), None, "tp"),
        P("tp"),
        P("tp", None, None),
        P(("dom", "grp")),
        P(("dom", "grp")),
        P(("dom", "grp")),
    )
    out_specs = P(("dom", "grp"), None, "tp", None)
    return jax.shard_map(body, mesh=mesh, in_specs=in_specs, out_specs=out_specs, check_vma=False)
```

```python
import functools

import jax
import jax.numpy as jnp
import numpy as np
from jax import lax
from jax.experimental import pallas as pl
from jax.experimental.pallas import tpu as pltpu
from jax.sharding import PartitionSpec as P

HD = 128
epsilon = 1e-05
MESH = pl.DeviceIdType.MESH


def exchange_kernel(
    groups, tps, own, heads, width,
    dest_ref, len_ref, start_ref, part_ref, hidden_ref, freq_ref,
    out_ref,
    sent, got, mixed, final, mark_s, mark_r, square_s, square_r, sums_s, sums_r, slot_sums, scales, cos_ref, sin_ref,
    s_send, s_recv, c_send, c_recv, m_send, m_recv, r_send, r_recv, q_send, q_recv,
):
    g = lax.axis_index("grp")
    z = lax.axis_index("tp")
    slots = part_ref.shape[1]
    blk = part_ref.shape[2]
    wide = part_ref.shape[3]
    units = sent.shape[1]
    cuts = units // heads
    rows = blk // cuts

    def over(n, body):
        lax.fori_loop(0, n, lambda i, c: (body(i), c)[1], 0)

    def grp_peer(k):
        return lax.rem(g + k + 1, groups)

    def tp_peer(k):
        side = lax.div(k + 1, 2) * (2 * lax.rem(k, 2) - 1)
        return lax.rem(z + tps // 2 + side, tps)

    barrier = pltpu.get_barrier_semaphore()

    @functools.partial(over, groups - 1)
    def _(k):
        pl.semaphore_signal(barrier, inc=1, device_id={"grp": grp_peer(k)}, device_id_type=MESH)

    @functools.partial(over, tps - 1)
    def _(k):
        pl.semaphore_signal(barrier, inc=1, device_id={"tp": tp_peer(k)}, device_id_type=MESH)

    def slot_of(owner):
        index, code = jnp.int32(0), jnp.int32(0)
        for s in range(slots):
            inner = dest_ref[s] - owner * own
            hit = (inner >= 0) & (inner < own)
            index = jnp.where(hit, s, index)
            code = jnp.where(hit, inner + 1, code)
        return index, code

    rows8 = lax.broadcasted_iota(jnp.int32, (8, wide), 0)

    def mark_of(owner):
        _, code = slot_of(owner)
        return jnp.full((8, wide), code.astype(jnp.float32))

    def block_copy(t, u, o, src_g):
        return pltpu.make_async_remote_copy(
            src_ref=sent.at[t, u, o], dst_ref=got.at[t, u, src_g],
            send_sem=s_send.at[t, u, o], recv_sem=s_recv.at[t, u, src_g],
            device_id={"grp": o}, device_id_type=MESH,
        )

    def mark_copy(o, src_g):
        return pltpu.make_async_remote_copy(
            src_ref=mark_s.at[o], dst_ref=mark_r.at[src_g],
            send_sem=m_send.at[o], recv_sem=m_recv.at[src_g],
            device_id={"grp": o}, device_id_type=MESH,
        )

    def square_copy(o, src_g):
        return pltpu.make_async_remote_copy(
            src_ref=square_s.at[o], dst_ref=square_r.at[src_g],
            send_sem=r_send.at[o], recv_sem=r_recv.at[src_g],
            device_id={"grp": o}, device_id_type=MESH,
        )

    def shard_copy(t, u, src_z):
        return pltpu.make_async_remote_copy(
            src_ref=mixed.at[t, u], dst_ref=final.at[src_z, u],
            send_sem=c_send.at[t, u], recv_sem=c_recv.at[src_z, u],
            device_id={"tp": t}, device_id_type=MESH,
        )

    def sums_copy(t, src_z):
        return pltpu.make_async_remote_copy(
            src_ref=sums_s, dst_ref=sums_r.at[src_z],
            send_sem=q_send.at[t], recv_sem=q_recv.at[src_z],
            device_id={"tp": t}, device_id_type=MESH,
        )

    mark_r[g] = mark_of(g)

    @functools.partial(over, groups - 1)
    def _(k):
        o = grp_peer(k)
        mark_s[o] = mark_of(o)

    pl.semaphore_wait(barrier, groups + tps - 2)

    @functools.partial(over, groups - 1)
    def _(k):
        mark_copy(grp_peer(k), g).start()

    mine, _ = slot_of(g)

    def send_blocks(t):
        @functools.partial(over, units)
        def _(u):
            head = t * heads + lax.div(u, cuts)
            span = pl.ds(pl.multiple_of(lax.rem(u, cuts) * rows, rows), rows)

            @functools.partial(over, groups - 1)
            def _(k):
                o = grp_peer(k)
                index, _ = slot_of(o)
                sent[t, u, o] = part_ref[head, index, span, :]
                block_copy(t, u, o, g).start()

            got[t, u, g] = part_ref[head, mine, span, :]

    send_blocks(tp_peer(0))

    lanes = HD
    step = 16

    @functools.partial(over, slots * (blk // step))
    def _(n):
        s = lax.div(n, blk // step)
        span = pl.ds(pl.multiple_of(lax.rem(n, blk // step) * step, step), step)
        totals = [jnp.zeros((step, lanes), jnp.float32)] * 2
        for c in range(width // lanes):
            x = hidden_ref[s, span, c * lanes : (c + 1) * lanes].astype(jnp.float32)
            totals[c % 2] = totals[c % 2] + x * x
        slot_sums[s, span, :] = totals[0] + totals[1]

    def squares_of(owner):
        index, _ = slot_of(owner)
        line = jnp.sum(jnp.transpose(slot_sums[index]), axis=0, keepdims=True)
        return jnp.broadcast_to(jnp.concatenate([line, line], axis=1), (8, wide))

    square_r[g] = squares_of(g)

    @functools.partial(over, groups - 1)
    def _(k):
        o = grp_peer(k)
        square_s[o] = squares_of(o)
        square_copy(o, g).start()

    send_blocks(tp_peer(1))

    @functools.partial(over, groups - 1)
    def _(k):
        o = grp_peer(k)
        mark_copy(o, o).wait_recv()

    def mix(t, u):
        @functools.partial(over, groups - 1)
        def _(k):
            o = grp_peer(k)
            block_copy(t, u, o, o).wait_recv()

        for j in range(own):
            def pick(s, total):
                marks = jnp.broadcast_to(mark_r[s, 0:1, :], (rows, wide))
                block = got[t, u, s].astype(jnp.float32)
                return total + jnp.where(marks == float(j + 1), block, 0.0)

            picked = lax.fori_loop(0, groups, pick, jnp.zeros((rows, wide), jnp.float32))
            mixed[t, u, j] = picked.astype(jnp.bfloat16)

    def mix_and_send(t):
        @functools.partial(over, units)
        def _(u):
            mix(t, u)
            shard_copy(t, u, z).start()

    mix_and_send(tp_peer(0))
    band = 32
    lane = lax.broadcasted_iota(jnp.int32, (band, HD), 1)
    offset = lax.broadcasted_iota(jnp.int32, (band, HD), 0)

    @functools.partial(over, own * (blk // band))
    def _(n):
        j = lax.div(n, blk // band)
        span = pl.ds(pl.multiple_of(lax.rem(n, blk // band) * band, band), band)
        positions = (offset + (start_ref[0] + n * band)).astype(jnp.float32)
        angles = positions * jnp.broadcast_to(freq_ref[0:1, :], (band, HD))
        sine = jnp.sin(angles)
        cos_ref[j, span, :] = jnp.cos(angles)
        sin_ref[j, span, :] = jnp.where(lane < HD // 2, -sine, sine)

    @functools.partial(over, groups - 1)
    def _(k):
        o = grp_peer(k)
        square_copy(o, o).wait_recv()

    def add_squares(s, total):
        same = mark_r[s] == (rows8 + 1).astype(jnp.float32)
        return total + jnp.where(same, square_r[s], 0.0)

    sums = lax.fori_loop(0, groups, add_squares, jnp.zeros((8, wide), jnp.float32))
    sums_s[...] = sums

    @functools.partial(over, tps - 1)
    def _(i):
        sums_copy(tp_peer(i), z).start()

    @functools.partial(over, tps - 2)
    def _(i):
        send_blocks(tp_peer(i + 2))
        mix_and_send(tp_peer(i + 1))

    @functools.partial(over, units)
    def _(u):
        mix(z, u)

    @functools.partial(over, tps - 1)
    def _(i):
        t = tp_peer(i)
        sums_copy(t, t).wait_recv()

    def add_sums(i, total):
        return total + sums_r[tp_peer(i)]

    total = lax.fori_loop(0, tps - 1, add_sums, sums)
    inverse = lax.rsqrt(total[:, :blk] / (width * tps) + epsilon)

    half = HD // 2
    token = lax.broadcasted_iota(jnp.int32, (rows, HD), 0)
    length = len_ref[0]
    for j in range(own):
        scales[j] = jnp.transpose(jnp.broadcast_to(inverse[j : j + 1, :], (blk, blk)))

    @functools.partial(over, units)
    def _(u):
        @functools.partial(over, tps - 1)
        def _(i):
            t = tp_peer(i)
            shard_copy(t, u, t).wait_recv()

        head = lax.div(u, cuts)
        first = pl.multiple_of(lax.rem(u, cuts) * rows, rows)
        span = pl.ds(first, rows)
        for j in range(own):
            live = token + (j * blk + first) < length

            def add(i, total):
                return total + final[tp_peer(i), u, j].astype(jnp.float32)

            raw = lax.fori_loop(0, tps - 1, add, mixed[z, u, j].astype(jnp.float32))
            scale = scales[j, span, :]
            key = raw[:, :HD] * scale
            value = raw[:, HD:] * scale
            swapped = pltpu.roll(key, half, 1)
            turned = key * cos_ref[j, span, :] + swapped * sin_ref[j, span, :]
            out_ref[j, head, span, :HD] = jnp.where(live, turned, 0.0).astype(out_ref.dtype)
            out_ref[j, head, span, HD:] = jnp.where(live, value, 0.0).astype(out_ref.dtype)

    @functools.partial(over, groups - 1)
    def _(k):
        o = grp_peer(k)
        mark_copy(o, g).wait_send()
        square_copy(o, g).wait_send()

    @functools.partial(over, tps)
    def _(t):
        @functools.partial(over, units)
        def _(u):
            @functools.partial(over, groups - 1)
            def _(k):
                block_copy(t, u, grp_peer(k), g).wait_send()

    @functools.partial(over, tps - 1)
    def _(i):
        t = tp_peer(i)
        sums_copy(t, z).wait_send()

        @functools.partial(over, units)
        def _(u):
            shard_copy(t, u, z).wait_send()


def frequencies():
    half = HD // 2
    freqs = np.exp(-np.log(500000.0) * (2.0 * np.arange(half) / HD))
    return jnp.asarray(np.tile(np.concatenate([freqs, freqs]), (8, 1)).astype(np.float32))


def body(hidden, norm_gain, kv_weight, dest_slot, session_len, session_start):
    groups, tps = lax.axis_size("grp"), lax.axis_size("tp")
    slots, blk, width = hidden.shape
    own = (3 * groups + 7) // 8
    heads = kv_weight.shape[1] // tps
    wide_cols = kv_weight.shape[2]
    wide = hidden.astype(jnp.float32)
    scaled = (wide * norm_gain[None, None, :]).astype(jnp.bfloat16).reshape(slots * blk, width)
    parts = jnp.einsum("rd,dhe->hre", scaled, kv_weight, preferred_element_type=jnp.float32)
    parts = parts.astype(jnp.bfloat16).reshape(kv_weight.shape[1], slots, blk, wide_cols)
    vmem = pl.BlockSpec(memory_space=pltpu.VMEM)
    smem = pl.BlockSpec(memory_space=pltpu.SMEM)
    cuts = 1
    units = heads * cuts
    piece = (blk // cuts, wide_cols)
    line = pltpu.VMEM((groups, 8, wide_cols), jnp.float32)
    table = pltpu.VMEM((own, blk, HD), jnp.float32)
    dma = pltpu.SemaphoreType.DMA
    out = pl.pallas_call(
        functools.partial(exchange_kernel, groups, tps, own, heads, width),
        out_shape=jax.ShapeDtypeStruct((own, heads, blk, wide_cols), jnp.bfloat16),
        in_specs=[smem, smem, smem, vmem, vmem, vmem],
        out_specs=vmem,
        scratch_shapes=[
            pltpu.VMEM((tps, units, groups) + piece, jnp.bfloat16),
            pltpu.VMEM((tps, units, groups) + piece, jnp.bfloat16),
            pltpu.VMEM((tps, units, own) + piece, jnp.bfloat16),
            pltpu.VMEM((tps, units, own) + piece, jnp.bfloat16),
            line, line, line, line,
            pltpu.VMEM((8, wide_cols), jnp.float32),
            pltpu.VMEM((tps, 8, wide_cols), jnp.float32),
            pltpu.VMEM((slots, blk, HD), jnp.float32),
            table, table, table,
            dma((tps, units, groups)), dma((tps, units, groups)),
            dma((tps, units)), dma((tps, units)),
            dma((groups,)), dma((groups,)),
            dma((groups,)), dma((groups,)),
            dma((tps,)), dma((tps,)),
        ],
        compiler_params=pltpu.CompilerParams(
            collective_id=0, has_side_effects=True, vmem_limit_bytes=40 * 1024 * 1024
        ),
        name="exchange",
    )(dest_slot, session_len, session_start, parts, hidden, frequencies())
    return jnp.transpose(out, (0, 2, 1, 3))


def solution(mesh):
    in_specs = (
        P(("dom", "grp"), None, "tp"),
        P("tp"),
        P("tp", None, None),
        P(("dom", "grp")),
        P(("dom", "grp")),
        P(("dom", "grp")),
    )
    out_specs = P(("dom", "grp"), None, "tp", None)
    return jax.shard_map(body, mesh=mesh, in_specs=in_specs, out_specs=out_specs, check_vma=False)
```

```python
import functools

import jax
import jax.numpy as jnp
import numpy as np
from jax import lax
from jax.experimental import pallas as pl
from jax.experimental.pallas import tpu as pltpu
from jax.sharding import PartitionSpec as P

HD = 128
epsilon = 1e-05
MESH = pl.DeviceIdType.MESH


def exchange_kernel(
    groups, tps, own, heads, width,
    dest_ref, len_ref, start_ref, part_ref, hidden_ref, freq_ref,
    out_ref,
    sent, got, mixed, final, mark_s, mark_r, square_s, square_r, sums_s, sums_r, slot_sums, scales, cos_ref, sin_ref,
    s_send, s_recv, c_send, c_recv, m_send, m_recv, r_send, r_recv, q_send, q_recv,
):
    g = lax.axis_index("grp")
    z = lax.axis_index("tp")
    slots = part_ref.shape[1]
    blk = part_ref.shape[2]
    wide = part_ref.shape[3]
    units = sent.shape[1]
    cuts = units // heads
    rows = blk // cuts

    def over(n, body):
        lax.fori_loop(0, n, lambda i, c: (body(i), c)[1], 0)

    def grp_peer(k):
        pair = lax.rem(lax.div(g, 2) + 1 + lax.div(k, 2), groups // 2)
        return 2 * pair + lax.rem(g + 1 + k, 2)

    def tp_peer(k):
        side = lax.div(k + 1, 2) * (2 * lax.rem(k, 2) - 1)
        return lax.rem(z + tps // 2 + side, tps)

    barrier = pltpu.get_barrier_semaphore()

    @functools.partial(over, groups - 1)
    def _(k):
        pl.semaphore_signal(barrier, inc=1, device_id={"grp": grp_peer(k)}, device_id_type=MESH)

    @functools.partial(over, tps - 1)
    def _(k):
        pl.semaphore_signal(barrier, inc=1, device_id={"tp": tp_peer(k)}, device_id_type=MESH)

    def slot_of(owner):
        index, code = jnp.int32(0), jnp.int32(0)
        for s in range(slots):
            inner = dest_ref[s] - owner * own
            hit = (inner >= 0) & (inner < own)
            index = jnp.where(hit, s, index)
            code = jnp.where(hit, inner + 1, code)
        return index, code

    rows8 = lax.broadcasted_iota(jnp.int32, (8, wide), 0)

    def mark_of(owner):
        _, code = slot_of(owner)
        return jnp.full((8, wide), code.astype(jnp.float32))

    def block_copy(t, u, o, src_g):
        return pltpu.make_async_remote_copy(
            src_ref=sent.at[t, u, o], dst_ref=got.at[t, u, src_g],
            send_sem=s_send.at[t, u, o], recv_sem=s_recv.at[t, u, src_g],
            device_id={"grp": o}, device_id_type=MESH,
        )

    def mark_copy(o, src_g):
        return pltpu.make_async_remote_copy(
            src_ref=mark_s.at[o], dst_ref=mark_r.at[src_g],
            send_sem=m_send.at[o], recv_sem=m_recv.at[src_g],
            device_id={"grp": o}, device_id_type=MESH,
        )

    def square_copy(o, src_g):
        return pltpu.make_async_remote_copy(
            src_ref=square_s.at[o], dst_ref=square_r.at[src_g],
            send_sem=r_send.at[o], recv_sem=r_recv.at[src_g],
            device_id={"grp": o}, device_id_type=MESH,
        )

    def shard_copy(t, u, src_z):
        return pltpu.make_async_remote_copy(
            src_ref=mixed.at[t, u], dst_ref=final.at[src_z, u],
            send_sem=c_send.at[t, u], recv_sem=c_recv.at[src_z, u],
            device_id={"tp": t}, device_id_type=MESH,
        )

    def sums_copy(t, src_z):
        return pltpu.make_async_remote_copy(
            src_ref=sums_s, dst_ref=sums_r.at[src_z],
            send_sem=q_send.at[t], recv_sem=q_recv.at[src_z],
            device_id={"tp": t}, device_id_type=MESH,
        )

    mark_r[g] = mark_of(g)

    @functools.partial(over, groups - 1)
    def _(k):
        o = grp_peer(k)
        mark_s[o] = mark_of(o)

    pl.semaphore_wait(barrier, groups + tps - 2)

    @functools.partial(over, groups - 1)
    def _(k):
        mark_copy(grp_peer(k), g).start()

    mine, _ = slot_of(g)

    def send_blocks(t):
        @functools.partial(over, units)
        def _(u):
            head = t * heads + lax.div(u, cuts)
            span = pl.ds(pl.multiple_of(lax.rem(u, cuts) * rows, rows), rows)

            @functools.partial(over, groups - 1)
            def _(k):
                o = grp_peer(k)
                index, _ = slot_of(o)
                sent[t, u, o] = part_ref[head, index, span, :]
                block_copy(t, u, o, g).start()

            got[t, u, g] = part_ref[head, mine, span, :]

    send_blocks(tp_peer(0))

    lanes = HD
    step = 16

    @functools.partial(over, slots * (blk // step))
    def _(n):
        s = lax.div(n, blk // step)
        span = pl.ds(pl.multiple_of(lax.rem(n, blk // step) * step, step), step)
        totals = [jnp.zeros((step, lanes), jnp.float32)] * 2
        for c in range(width // lanes):
            x = hidden_ref[s, span, c * lanes : (c + 1) * lanes].astype(jnp.float32)
            totals[c % 2] = totals[c % 2] + x * x
        slot_sums[s, span, :] = totals[0] + totals[1]

    def squares_of(owner):
        index, _ = slot_of(owner)
        line = jnp.sum(jnp.transpose(slot_sums[index]), axis=0, keepdims=True)
        return jnp.broadcast_to(jnp.concatenate([line, line], axis=1), (8, wide))

    square_r[g] = squares_of(g)

    @functools.partial(over, groups - 1)
    def _(k):
        o = grp_peer(k)
        square_s[o] = squares_of(o)
        square_copy(o, g).start()

    send_blocks(tp_peer(1))

    @functools.partial(over, groups - 1)
    def _(k):
        o = grp_peer(k)
        mark_copy(o, o).wait_recv()

    def mix(t, u):
        @functools.partial(over, groups - 1)
        def _(k):
            o = grp_peer(k)
            block_copy(t, u, o, o).wait_recv()

        for j in range(own):
            def pick(s, total):
                marks = jnp.broadcast_to(mark_r[s, 0:1, :], (rows, wide))
                block = got[t, u, s].astype(jnp.float32)
                return total + jnp.where(marks == float(j + 1), block, 0.0)

            picked = lax.fori_loop(0, groups, pick, jnp.zeros((rows, wide), jnp.float32))
            mixed[t, u, j] = picked.astype(jnp.bfloat16)

    def mix_and_send(t):
        @functools.partial(over, units)
        def _(u):
            mix(t, u)
            shard_copy(t, u, z).start()

    mix_and_send(tp_peer(0))
    band = 32
    lane = lax.broadcasted_iota(jnp.int32, (band, HD), 1)
    offset = lax.broadcasted_iota(jnp.int32, (band, HD), 0)

    @functools.partial(over, own * (blk // band))
    def _(n):
        j = lax.div(n, blk // band)
        span = pl.ds(pl.multiple_of(lax.rem(n, blk // band) * band, band), band)
        positions = (offset + (start_ref[0] + n * band)).astype(jnp.float32)
        angles = positions * jnp.broadcast_to(freq_ref[0:1, :], (band, HD))
        sine = jnp.sin(angles)
        cos_ref[j, span, :] = jnp.cos(angles)
        sin_ref[j, span, :] = jnp.where(lane < HD // 2, -sine, sine)

    @functools.partial(over, groups - 1)
    def _(k):
        o = grp_peer(k)
        square_copy(o, o).wait_recv()

    def add_squares(s, total):
        same = mark_r[s] == (rows8 + 1).astype(jnp.float32)
        return total + jnp.where(same, square_r[s], 0.0)

    sums = lax.fori_loop(0, groups, add_squares, jnp.zeros((8, wide), jnp.float32))
    sums_s[...] = sums

    @functools.partial(over, tps - 1)
    def _(i):
        sums_copy(tp_peer(i), z).start()

    @functools.partial(over, tps - 2)
    def _(i):
        send_blocks(tp_peer(i + 2))
        mix_and_send(tp_peer(i + 1))

    @functools.partial(over, units)
    def _(u):
        mix(z, u)

    @functools.partial(over, tps - 1)
    def _(i):
        t = tp_peer(i)
        sums_copy(t, t).wait_recv()

    def add_sums(i, total):
        return total + sums_r[tp_peer(i)]

    total = lax.fori_loop(0, tps - 1, add_sums, sums)
    inverse = lax.rsqrt(total[:, :blk] / (width * tps) + epsilon)

    half = HD // 2
    token = lax.broadcasted_iota(jnp.int32, (rows, HD), 0)
    length = len_ref[0]
    for j in range(own):
        scales[j] = jnp.transpose(jnp.broadcast_to(inverse[j : j + 1, :], (blk, blk)))

    @functools.partial(over, units)
    def _(u):
        @functools.partial(over, tps - 1)
        def _(i):
            t = tp_peer(i)
            shard_copy(t, u, t).wait_recv()

        head = lax.div(u, cuts)
        first = pl.multiple_of(lax.rem(u, cuts) * rows, rows)
        span = pl.ds(first, rows)
        for j in range(own):
            live = token + (j * blk + first) < length

            def add(i, total):
                return total + final[tp_peer(i), u, j].astype(jnp.float32)

            raw = lax.fori_loop(0, tps - 1, add, mixed[z, u, j].astype(jnp.float32))
            scale = scales[j, span, :]
            key = raw[:, :HD] * scale
            value = raw[:, HD:] * scale
            swapped = pltpu.roll(key, half, 1)
            turned = key * cos_ref[j, span, :] + swapped * sin_ref[j, span, :]
            out_ref[j, head, span, :HD] = jnp.where(live, turned, 0.0).astype(out_ref.dtype)
            out_ref[j, head, span, HD:] = jnp.where(live, value, 0.0).astype(out_ref.dtype)

    @functools.partial(over, groups - 1)
    def _(k):
        o = grp_peer(k)
        mark_copy(o, g).wait_send()
        square_copy(o, g).wait_send()

    @functools.partial(over, tps)
    def _(t):
        @functools.partial(over, units)
        def _(u):
            @functools.partial(over, groups - 1)
            def _(k):
                block_copy(t, u, grp_peer(k), g).wait_send()

    @functools.partial(over, tps - 1)
    def _(i):
        t = tp_peer(i)
        sums_copy(t, z).wait_send()

        @functools.partial(over, units)
        def _(u):
            shard_copy(t, u, z).wait_send()


def frequencies():
    half = HD // 2
    freqs = np.exp(-np.log(500000.0) * (2.0 * np.arange(half) / HD))
    return jnp.asarray(np.tile(np.concatenate([freqs, freqs]), (8, 1)).astype(np.float32))


def body(hidden, norm_gain, kv_weight, dest_slot, session_len, session_start):
    groups, tps = lax.axis_size("grp"), lax.axis_size("tp")
    slots, blk, width = hidden.shape
    own = (3 * groups + 7) // 8
    heads = kv_weight.shape[1] // tps
    wide_cols = kv_weight.shape[2]
    wide = hidden.astype(jnp.float32)
    scaled = (wide * norm_gain[None, None, :]).astype(jnp.bfloat16).reshape(slots * blk, width)
    parts = jnp.einsum("rd,dhe->hre", scaled, kv_weight, preferred_element_type=jnp.float32)
    parts = parts.astype(jnp.bfloat16).reshape(kv_weight.shape[1], slots, blk, wide_cols)
    vmem = pl.BlockSpec(memory_space=pltpu.VMEM)
    smem = pl.BlockSpec(memory_space=pltpu.SMEM)
    cuts = 1
    units = heads * cuts
    piece = (blk // cuts, wide_cols)
    line = pltpu.VMEM((groups, 8, wide_cols), jnp.float32)
    table = pltpu.VMEM((own, blk, HD), jnp.float32)
    dma = pltpu.SemaphoreType.DMA
    out = pl.pallas_call(
        functools.partial(exchange_kernel, groups, tps, own, heads, width),
        out_shape=jax.ShapeDtypeStruct((own, heads, blk, wide_cols), jnp.bfloat16),
        in_specs=[smem, smem, smem, vmem, vmem, vmem],
        out_specs=vmem,
        scratch_shapes=[
            pltpu.VMEM((tps, units, groups) + piece, jnp.bfloat16),
            pltpu.VMEM((tps, units, groups) + piece, jnp.bfloat16),
            pltpu.VMEM((tps, units, own) + piece, jnp.bfloat16),
            pltpu.VMEM((tps, units, own) + piece, jnp.bfloat16),
            line, line, line, line,
            pltpu.VMEM((8, wide_cols), jnp.float32),
            pltpu.VMEM((tps, 8, wide_cols), jnp.float32),
            pltpu.VMEM((slots, blk, HD), jnp.float32),
            table, table, table,
            dma((tps, units, groups)), dma((tps, units, groups)),
            dma((tps, units)), dma((tps, units)),
            dma((groups,)), dma((groups,)),
            dma((groups,)), dma((groups,)),
            dma((tps,)), dma((tps,)),
        ],
        compiler_params=pltpu.CompilerParams(
            collective_id=0, has_side_effects=True, vmem_limit_bytes=40 * 1024 * 1024
        ),
        name="exchange",
    )(dest_slot, session_len, session_start, parts, hidden, frequencies())
    return jnp.transpose(out, (0, 2, 1, 3))


def solution(mesh):
    in_specs = (
        P(("dom", "grp"), None, "tp"),
        P("tp"),
        P("tp", None, None),
        P(("dom", "grp")),
        P(("dom", "grp")),
        P(("dom", "grp")),
    )
    out_specs = P(("dom", "grp"), None, "tp", None)
    return jax.shard_map(body, mesh=mesh, in_specs=in_specs, out_specs=out_specs, check_vma=False)
```
